32 devices in a mesh: gx: 4 (over x, core), gy: 4 (over z), gz: 2 (over y).
Axes of the slice: x: 2, y: 2, z: 4, core: 2. Of those that a mesh axis runs over, the one named last changes fastest.
Arguments:
- velocity: float32 [3, 512, 128, 128], P(None, 'gx', 'gy', 'gz'), may hold values from -6 to 6
- window_offsets: int32 [4, 4], replicated, may hold values from 0 to 31
- window_counts: int32 [4], replicated, may hold values from 1 to 4, as said below
- lift_weight: float32 [64, 3], replicated, may hold values from -3.5 to 3.5
- spectral_weight: bfloat16 [2, 256, 16, 64, 64], P(None, ('gy', 'gz')), may hold values from -6 to 6
- point_weight: float32 [64, 64], replicated, may hold values from -0.75 to 0.75
- proj_weight: float32 [3, 64], replicated, may hold values from -0.75 to 0.75
Outputs:
- velocity_next: float32 [3, 512, 128, 128], P(None, 'gx', 'gy', 'gz')
- grad_spectral: float32 [2, 256, 16, 64, 64], P(None, ('gy', 'gz'))
The draws below stay inside these ranges and needn't reach their ends.
Inputs may be any that keep to these rules, and one draw needn't show every extreme that they name: `window_counts`: at least one group has all 4 slots live.
All inputs are finite; a program needn't handle non-finite values.
Results may differ from the reference program's by a relative error of at most 0.0003.
Values sent between devices are 32-bit elements; how exact they have to be, the bound alone decides.
A program may use at most 320 MiB of HBM per device.

```python
import math
import jax
import jax.numpy as jnp
from jax import lax

W = 64
KM = 16
WIN = 32
RATIO = 4
CZ = 64
SLOTS = 4
NX = 512
NY = 128
NZ = 128
KX = 16
KYZ = 256
N_GX = 4
N_GZ = 2


def draw_window_counts(key, part):
    key = jax.random.fold_in(key, 11)
    key_counts, key_fullest = jax.random.split(key)
    counts = jax.random.randint(key_counts, (N_GX,), 1, SLOTS + 1)
    fullest = jax.random.randint(key_fullest, (), 0, N_GX)
    return jnp.where(jnp.arange(N_GX) == fullest, SLOTS, counts).astype(jnp.int32)


def touch_ends(values, key, low, largest):
    shape = values.shape
    index_at = [jax.random.randint(jax.random.fold_in(key, axis), (), 0, shape[axis]) for axis in range(len(shape))]
    values = values.at[tuple(index_at)].set(low)
    longest = shape.index(max(shape))
    index_at[longest] = (index_at[longest] + 1) % shape[longest]
    return values.at[tuple(index_at)].set(largest)


def levels(stream_key, extent, pieces, low, largest):
    loudness, own = 1.0, jax.random.fold_in(stream_key, 6)
    for dim, parts in pieces:
        steps = jnp.exp(jax.random.uniform(jax.random.fold_in(own, dim), (parts,), jnp.float32, low / len(pieces), largest / len(pieces)))
        loudness = loudness * jnp.repeat(steps, extent[dim] // parts).reshape([-1 if axis == dim else 1 for axis in range(len(extent))])
    return loudness


def scatter_about(own_key, shape, width, reach, cuts=(), kind=jnp.bfloat16):
    level = levels(own_key, shape, cuts, -0.22, 0.18) if cuts else 1.0
    result = jax.random.normal(own_key, shape, jnp.float32) * width * level
    return jnp.minimum(jnp.maximum(result, -reach), reach).astype(kind)


def setup_inputs(seed: int = 0) -> dict:
    key_of = jax.random.split(jax.random.key(seed), 8)
    velocity = scatter_about(key_of[0], (3, NX, NY, NZ), 1.0, 6.0, ((1, 4), (2, 4), (3, 2)), jnp.float32)
    window_offsets = touch_ends(jax.random.randint(key_of[1], (N_GX, SLOTS), 0, CZ * N_GZ // RATIO), jax.random.fold_in(key_of[1], 1), 0, (CZ * N_GZ // RATIO) - 1).astype(jnp.int32)
    window_counts = draw_window_counts(jax.random.fold_in(key_of[7], 71), 0)
    lift_weight = scatter_about(key_of[3], (W, 3), 3 ** -0.5, 3.5, (), jnp.float32)
    spectral_weight = scatter_about(key_of[4], (2, KYZ, KX, W, W), 1.0, 6.0, ((1, 8),))
    point_weight = scatter_about(key_of[5], (W, W), W ** -0.5, 0.75, (), jnp.float32)
    proj_weight = scatter_about(key_of[6], (3, W), W ** -0.5, 0.75, (), jnp.float32)
    return dict(velocity=velocity, window_offsets=window_offsets, window_counts=window_counts, lift_weight=lift_weight, spectral_weight=spectral_weight, point_weight=point_weight, proj_weight=proj_weight)


time_step = 0.1
viscosity = 1.0
highest = lax.Precision.HIGHEST

def advance_component(center, itself, upper_side, lower_side):
    laplace = upper_side[0] + lower_side[0] + upper_side[1] + lower_side[1] + upper_side[2] + lower_side[2] - 6.0 * itself
    carried = center[0] * (upper_side[0] - lower_side[0]) + center[1] * (upper_side[1] - lower_side[1]) + center[2] * (upper_side[2] - lower_side[2])
    return itself + time_step * (viscosity * laplace - 0.5 * carried)

def coarsen_field(field, ratio):
    comps, size_x, size_y, size_z = field.shape
    blocks = field.reshape(comps, size_x // ratio, ratio, size_y // ratio, ratio, size_z // ratio, ratio)
    return lax.optimization_barrier(jnp.mean(blocks, axis=(2, 4, 6)))

def fourier_table(length, modes):
    points = jnp.arange(length, dtype=jnp.int32)
    freqs = jnp.arange(modes, dtype=jnp.int32) - modes // 2
    phase = points[:, None] * freqs[None, :] % length
    angle = 2.0 * math.pi / length * phase.astype(jnp.float32)
    return (jnp.cos(angle), jnp.sin(angle))

def rotate_axis(real_part, imag_part, cosine_table, sine_table, which_axis, orientation, keep_imag=True):

    def contract(values, factor_table):
        product = jnp.tensordot(values, factor_table, axes=([which_axis], [0]), precision=highest)
        return jnp.moveaxis(product, -1, which_axis)
    if imag_part is None:
        return (contract(real_part, cosine_table), orientation * contract(real_part, sine_table))
    new_real = contract(real_part, cosine_table) - orientation * contract(imag_part, sine_table)
    if not keep_imag:
        return new_real
    new_imag = orientation * contract(real_part, sine_table) + contract(imag_part, cosine_table)
    return (new_real, new_imag)

def forward_yz(field, cosine_table, sine_table):
    real_part, imag_part = rotate_axis(field, None, cosine_table, sine_table, 4, -1.0)
    return rotate_axis(real_part, imag_part, cosine_table, sine_table, 3, -1.0)

def windows_of(field, offsets, length):
    zlength = field.shape[-1]
    index = (offsets[:, None] + jnp.arange(length, dtype=jnp.int32)[None, :]) % zlength
    picked = jnp.take(field, index.astype(jnp.int32), axis=3)
    return jnp.transpose(picked, (3, 0, 1, 2, 4))

def reference(velocity, window_offsets, window_counts, lift_weight, spectral_weight, point_weight, proj_weight):
    center = velocity
    results = []
    for component in range(3):
        itself = velocity[component]
        upper_side = [jnp.roll(itself, -1, axis=dim_index) for dim_index in range(3)]
        lower_side = [jnp.roll(itself, 1, axis=dim_index) for dim_index in range(3)]
        results.append(advance_component(center, itself, upper_side, lower_side))
    velocity_next = jnp.stack(results)
    coarse_old = coarsen_field(velocity, RATIO)
    coarse_new = coarsen_field(velocity_next, RATIO)
    cosine_table, sine_table = fourier_table(WIN, KM)
    scaling = float(WIN) ** (-1.5)
    weights = spectral_weight.astype(jnp.float32).reshape(2, KM, KM, KM, W, W)

    def group_grad(carry, group):
        start = (group * WIN).astype(jnp.int32)
        region_old = lax.dynamic_slice_in_dim(coarse_old, start, WIN, 1)
        region_new = lax.dynamic_slice_in_dim(coarse_new, start, WIN, 1)
        offsets = window_offsets[group]
        count = window_counts[group]
        inputs = windows_of(region_old, offsets, WIN)
        targets = windows_of(region_new, offsets, WIN)
        hidden = jnp.einsum('wc,scxyz->swxyz', lift_weight, inputs, precision=highest)
        mode_real, mode_imag = forward_yz(hidden, cosine_table, sine_table)
        mode_real, mode_imag = rotate_axis(mode_real, mode_imag, cosine_table, sine_table, 2, -1.0)
        mode_real = mode_real * scaling
        mode_imag = mode_imag * scaling
        pointwise = jnp.einsum('oi,sixyz->soxyz', point_weight, hidden, precision=highest)
        live = (jnp.arange(inputs.shape[0], dtype=jnp.int32) < count).astype(jnp.float32)

        def loss_of(mixing):
            weight_real = mixing[0]
            weight_imag = mixing[1]
            mixed_real = jnp.einsum('sixyz,yzxio->soxyz', mode_real, weight_real, precision=highest) - jnp.einsum('sixyz,yzxio->soxyz', mode_imag, weight_imag, precision=highest)
            mixed_imag = jnp.einsum('sixyz,yzxio->soxyz', mode_imag, weight_real, precision=highest) + jnp.einsum('sixyz,yzxio->soxyz', mode_real, weight_imag, precision=highest)
            back_real, back_imag = rotate_axis(mixed_real, mixed_imag, cosine_table.T, sine_table.T, 2, 1.0)
            back_real, back_imag = rotate_axis(back_real, back_imag, cosine_table.T, sine_table.T, 3, 1.0)
            spectral = rotate_axis(back_real, back_imag, cosine_table.T, sine_table.T, 4, 1.0, False) * scaling
            act = jax.nn.gelu(spectral + pointwise, approximate=False)
            output = jnp.einsum('co,soxyz->scxyz', proj_weight, act, precision=highest)
            differ = output - targets
            return 0.5 * jnp.sum(live[:, None, None, None, None] * differ * differ)
        return (carry + jax.grad(loss_of)(weights), None)
    total, unused = lax.scan(group_grad, jnp.zeros(weights.shape, jnp.float32), jnp.arange(N_GX, dtype=jnp.int32))
    grad_spectral = total.reshape(2, KM * KM, KM, W, W)
    return (velocity_next, grad_spectral)
```

```python
import functools
import math

import jax
import jax.numpy as jnp
import ml_dtypes
import numpy as np
from jax import lax
from jax.experimental import pallas as pl
from jax.experimental.pallas import tpu as pltpu
from jax.sharding import PartitionSpec as P

KM = 16
WIN = 32
RATIO = 4

time_step = 0.1
viscosity = 1.0
highest = lax.Precision.HIGHEST


def fourier_angles():
    points = np.arange(WIN)
    freqs = np.arange(KM) - KM // 2
    return 2.0 * math.pi / WIN * ((points[:, None] * freqs[None, :]) % WIN)


def plane_table(parts):
    angle = fourier_angles()
    full = angle.T[:, None, None, :] + angle.T[None, :, :, None]
    full = full.reshape(parts, 1, KM * KM // parts, WIN * WIN)
    both = np.concatenate([np.cos(full), -np.sin(full)], axis=1) * float(WIN) ** (-1.5)
    return both.reshape(2 * KM * KM, WIN * WIN).astype(np.float32)


def line_table():
    angle = fourier_angles()
    table = np.zeros((WIN, 2, KM, 2))
    table[:, 0, :, 0] = np.cos(angle)
    table[:, 0, :, 1] = -np.sin(angle)
    table[:, 1, :, 0] = np.sin(angle)
    table[:, 1, :, 1] = np.cos(angle)
    return table.astype(np.float32)


def halves(table):
    high = table.astype(ml_dtypes.bfloat16)
    low = (table - high.astype(np.float32)).astype(ml_dtypes.bfloat16)
    return jnp.asarray(high), jnp.asarray(low)


def split(values):
    high = values.astype(jnp.bfloat16)
    low = (values - high.astype(jnp.float32)).astype(jnp.bfloat16)
    return high, low


def mul(a, b):
    return jnp.dot(a, b, preferred_element_type=jnp.float32)


def stencil_body(v_ref, x_ref, y_ref, z_ref, out_ref):
    planes = v_ref.shape[1]

    def plane(x, before, after):
        center = [v_ref[c, x] for c in range(3)]
        for c in range(3):
            u = center[c]
            upper = [after(c), jnp.concatenate([u[1:], y_ref[c, x, 1:2]], axis=0),
                     jnp.concatenate([u[:, 1:], z_ref[c, x, :, 1:2]], axis=1)]
            lower = [before(c), jnp.concatenate([y_ref[c, x, 0:1], u[:-1]], axis=0),
                     jnp.concatenate([z_ref[c, x, :, 0:1], u[:, :-1]], axis=1)]
            laplace = upper[0] + lower[0] + upper[1] + lower[1] + upper[2] + lower[2] - 6.0 * u
            carried = (center[0] * (upper[0] - lower[0]) + center[1] * (upper[1] - lower[1])
                       + center[2] * (upper[2] - lower[2]))
            out_ref[c, x] = u + time_step * (viscosity * laplace - 0.5 * carried)

    plane(0, lambda c: x_ref[c, 0], lambda c: v_ref[c, 1])

    def step(x, carry):
        plane(x, lambda c: v_ref[c, x - 1], lambda c: v_ref[c, x + 1])
        return carry

    lax.fori_loop(1, planes - 1, step, 0)
    plane(planes - 1, lambda c: v_ref[c, planes - 2], lambda c: x_ref[c, 1])


def mix_body(h_ref, w_ref, out_ref):
    for k in range(KM):
        h = h_ref[0, k]
        rows = h.shape[0]
        high = h.astype(jnp.bfloat16).astype(jnp.float32)
        lhs = jnp.concatenate([high, h - high], axis=0).astype(jnp.bfloat16)
        weight = jnp.concatenate([w_ref[0, 0, k], w_ref[1, 0, k]], axis=0)
        both = mul(lhs, weight)
        out_ref[0, k] = both[:rows] + both[rows:]


def middle_body(slots, b_ref, inp_ref, tgt_ref, live_ref, m1_ref, p1_ref, p2_ref,
                bh_ref, bl_ref, fh_ref, fl_ref, out_ref):
    blocks, _, two, modes, lanes = b_ref.shape
    b = b_ref[...].reshape(blocks * two * modes, lanes)
    high, low = split(b)
    pre = mul(bh_ref[...], high) + mul(bh_ref[...], low) + mul(bl_ref[...], high)
    pre = pre + jnp.dot(inp_ref[0], m1_ref[...], precision=highest,
                        preferred_element_type=jnp.float32)
    cdf = 0.5 + 0.5 * lax.erf(pre * math.sqrt(0.5))
    act = pre * cdf
    slope = cdf + pre * (jnp.exp(-0.5 * pre * pre) * (1.0 / math.sqrt(2.0 * math.pi)))
    output = jnp.dot(act, p1_ref[...], precision=highest, preferred_element_type=jnp.float32)
    error = (output - tgt_ref[0]) * live_ref[...]
    grad = jnp.dot(error, p2_ref[...], precision=highest,
                   preferred_element_type=jnp.float32) * slope
    high, low = split(grad)
    cot = mul(fh_ref[...], high) + mul(fh_ref[...], low) + mul(fl_ref[...], high)
    out_ref[...] = cot.reshape(b_ref.shape)


def grad_body(a_ref, b_ref, out_ref):
    for k in range(KM):
        a = a_ref[0, k]
        depth = a.shape[1] // 3
        high = a.astype(jnp.bfloat16).astype(jnp.float32)
        lane = lax.broadcasted_iota(jnp.int32, a.shape, 1)
        middle = (lane >= depth) & (lane < 2 * depth)
        lhs = jnp.where(middle, a - high, high).astype(jnp.bfloat16)
        b = b_ref[0, k]
        half = depth // 2
        bh = b.astype(jnp.bfloat16).astype(jnp.float32)
        bl = b - bh
        first = jnp.concatenate([bh, bh, bl], axis=0).astype(jnp.bfloat16)
        th = jnp.concatenate([bh[half:], -bh[:half]], axis=0)
        tl = jnp.concatenate([bl[half:], -bl[:half]], axis=0)
        second = jnp.concatenate([th, th, tl], axis=0).astype(jnp.bfloat16)
        out_ref[0, 0, k] = mul(lhs, first)
        out_ref[1, 0, k] = mul(lhs, second)


def around(x, axis, dim):
    size, length = lax.axis_size(axis), x.shape[dim]
    up = [(i, (i + 1) % size) for i in range(size)]
    down = [(j, i) for i, j in up]
    last = lax.squeeze(lax.slice_in_dim(x, length - 1, length, axis=dim), (dim,))
    first = lax.squeeze(lax.slice_in_dim(x, 0, 1, axis=dim), (dim,))
    return lax.ppermute(last, axis, up), lax.ppermute(first, axis, down)


def coarsen(field):
    comps, nx, ny, nz = field.shape
    lines = field.reshape(comps, nx // RATIO, RATIO, ny, nz).sum(axis=2)
    sum_z = jnp.asarray(np.kron(np.eye(nz // RATIO), np.ones((RATIO, 1))).astype(np.float32))
    sum_y = jnp.asarray(
        np.kron(np.eye(ny // RATIO), np.ones((RATIO, 1))).astype(np.float32) / RATIO**3)
    lines = jnp.einsum("axyz,zv->axyv", lines, sum_z, precision=highest)
    return jnp.einsum("axyv,yu->vuax", lines, sum_y, precision=highest)


def windows(field, offsets, slots):
    longer = jnp.concatenate([field, field[:WIN]], axis=0)
    return jnp.stack(
        [lax.dynamic_slice_in_dim(longer, offsets[s], WIN, 0) for s in range(slots)])


def local(
    velocity, window_offsets, window_counts, lift_weight, spectral_weight, point_weight, proj_weight
):
    both_axes = ("gy", "gz")
    rows_y, rows_z, groups = lax.axis_size("gy"), lax.axis_size("gz"), lax.axis_size("gx")
    parts = rows_y * rows_z
    part = lax.axis_index("gy") * rows_z + lax.axis_index("gz")
    group = lax.axis_index("gx")
    slots = window_offsets.shape[1]
    width = lift_weight.shape[0]
    lanes = slots * width
    modes = spectral_weight.shape[1]
    planes = WIN // parts
    cells = WIN * WIN
    offsets = lax.dynamic_index_in_dim(window_offsets, group, 0, keepdims=False)
    count = lax.dynamic_index_in_dim(window_counts, group, 0, keepdims=False)
    live = (jnp.arange(slots, dtype=jnp.int32) < count).astype(jnp.float32)
    big = pltpu.CompilerParams(vmem_limit_bytes=48 * 1024 * 1024)
    table = plane_table(parts)
    line = jnp.asarray(line_table())

    old = coarsen(velocity)
    zl, yl, comps, _ = old.shape
    old = lax.all_gather(old.reshape(zl, yl, comps * WIN), both_axes)
    old = old.reshape(rows_y, rows_z, zl, yl, comps * WIN)
    old = jnp.transpose(old, (1, 2, 0, 3, 4)).reshape(rows_z * zl, rows_y * yl, comps * WIN)
    seen = windows(old, offsets, slots).reshape(slots, cells, comps * WIN)
    mine = lax.dynamic_index_in_dim(
        jnp.asarray(table).reshape(parts, 2 * modes, cells), part, 0, keepdims=False)
    inner = jnp.einsum("qn,snr->sqr", mine, seen, precision=highest)
    inner = inner.reshape(slots, 2, modes, comps, WIN)
    found = jnp.einsum("xckd,scmax->mkdsa", line, inner, precision=highest)
    found = found.reshape(modes * KM * 2 * slots, comps)
    hid = jnp.einsum("ra,wa->rw", found, lift_weight, precision=highest)
    hid = hid.reshape(modes, KM, 2, slots, width)
    lhs = jnp.concatenate(
        [
            jnp.concatenate([hid[:, :, 0], -hid[:, :, 1]], axis=-1),
            jnp.concatenate([hid[:, :, 1], hid[:, :, 0]], axis=-1),
        ],
        axis=2,
    )
    mixed = pl.pallas_call(
        mix_body,
        grid=(modes,),
        in_specs=[
            pl.BlockSpec((1, KM, 2 * slots, 2 * width), lambda i: (i, 0, 0, 0)),
            pl.BlockSpec((2, 1, KM, width, width), lambda i: (0, i, 0, 0, 0)),
        ],
        out_specs=pl.BlockSpec((1, KM, 2 * slots, width), lambda i: (i, 0, 0, 0)),
        out_shape=jax.ShapeDtypeStruct((modes, KM, 2 * slots, width), jnp.float32),
        compiler_params=big,
    )(lhs, spectral_weight)
    mixed = mixed.reshape(modes, KM, 2, slots, width)
    mixed = jnp.transpose(mixed, (1, 2, 0, 3, 4)).reshape(2 * KM, modes * lanes)
    flat = line.reshape(2 * WIN, 2 * KM)
    back = jnp.dot(flat, mixed, precision=highest)
    back = back.reshape(parts, planes, 2, modes, lanes)
    back = lax.all_to_all(back, both_axes, split_axis=0, concat_axis=0, tiled=True)

    x_side = jnp.stack(around(velocity, "gx", 1), axis=1)
    y_side = jnp.stack(around(velocity, "gy", 2), axis=2)
    z_side = jnp.stack(around(velocity, "gz", 3), axis=3)
    velocity_next = pl.pallas_call(
        stencil_body,
        out_shape=jax.ShapeDtypeStruct(velocity.shape, jnp.float32),
        in_specs=[pl.BlockSpec(memory_space=pltpu.VMEM)] * 4,
        out_specs=pl.BlockSpec(memory_space=pltpu.VMEM),
        compiler_params=big,
        cost_estimate=pl.CostEstimate(
            flops=20 * velocity.size, bytes_accessed=16 * velocity.size, transcendentals=0),
    )(velocity, x_side, y_side, z_side)
    new = coarsen(velocity_next)
    new = new.reshape(zl, yl, comps, parts, planes)
    new = jnp.transpose(new, (3, 0, 1, 2, 4)).reshape(parts, zl, yl, comps * planes)
    new = lax.all_to_all(new, both_axes, split_axis=0, concat_axis=0, tiled=True)
    new = new.reshape(rows_y, rows_z, zl, yl, comps * planes)
    new = jnp.transpose(new, (1, 2, 0, 3, 4)).reshape(rows_z * zl, rows_y * yl, comps * planes)

    def by_plane(values):
        values = values.reshape(slots, cells, comps, planes)
        return jnp.transpose(values, (3, 1, 0, 2)).reshape(planes, cells, slots * comps)

    targets = by_plane(windows(new, offsets, slots))
    own = lax.dynamic_slice_in_dim(
        seen.reshape(slots, cells, comps, WIN), part * planes, planes, 3)
    inputs = by_plane(own)

    eye = jnp.eye(slots, dtype=jnp.float32)
    point = jnp.dot(point_weight, lift_weight, precision=highest)
    m1 = jnp.einsum("st,oc->scto", eye, point, precision=highest).reshape(slots * comps, lanes)
    p2 = jnp.einsum("st,co->scto", eye, proj_weight, precision=highest)
    p2 = p2.reshape(slots * comps, lanes)
    alive = jnp.repeat(live, comps)[None]
    forward_high, forward_low = halves(table)
    back_high, back_low = halves(np.ascontiguousarray(table.T))

    def whole(shape):
        return pl.BlockSpec(shape, lambda i: (0,) * len(shape))

    sc = slots * comps
    plane_spec = pl.BlockSpec((1, cells, sc), lambda i: (i, 0, 0))
    mode_spec = pl.BlockSpec((parts, 1, 2, modes, lanes), lambda i: (0, i, 0, 0, 0))
    full_modes = 2 * modes * parts
    cot = pl.pallas_call(
        functools.partial(middle_body, slots),
        grid=(planes,),
        in_specs=[
            mode_spec, plane_spec, plane_spec, whole((1, sc)), whole((sc, lanes)),
            whole((lanes, sc)), whole((sc, lanes)), whole((cells, full_modes)),
            whole((cells, full_modes)), whole((full_modes, cells)), whole((full_modes, cells)),
        ],
        out_specs=mode_spec,
        out_shape=jax.ShapeDtypeStruct(back.shape, jnp.float32),
        compiler_params=big,
    )(back, inputs, targets, alive, m1, p2.T, p2, back_high, back_low, forward_high, forward_low)
    cot = lax.all_to_all(cot, both_axes, split_axis=0, concat_axis=0, tiled=True)
    cot = jnp.dot(flat.T, cot.reshape(2 * WIN, modes * lanes), precision=highest)

    every = lax.all_gather(found.reshape(modes, KM, 2, slots, comps), "gx")
    left = jnp.einsum("gmkdsa,wa->mkwdgs", every, lift_weight, precision=highest)
    depth = 2 * groups * slots
    left = left.reshape(modes, KM, width, depth)
    left = jnp.concatenate([left, left, left], axis=-1)
    right = lax.all_gather(cot, "gx").reshape(groups, KM, 2, modes, slots, width)
    right = jnp.transpose(right, (3, 1, 2, 0, 4, 5)).reshape(modes, KM, depth, width)
    grad_spectral = pl.pallas_call(
        grad_body,
        grid=(modes,),
        in_specs=[
            pl.BlockSpec((1, KM, width, 3 * depth), lambda i: (i, 0, 0, 0)),
            pl.BlockSpec((1, KM, depth, width), lambda i: (i, 0, 0, 0)),
        ],
        out_specs=pl.BlockSpec((2, 1, KM, width, width), lambda i: (0, i, 0, 0, 0)),
        out_shape=jax.ShapeDtypeStruct((2, modes, KM, width, width), jnp.float32),
        compiler_params=big,
    )(left, right)
    return (velocity_next, grad_spectral)


def solution(mesh):
    placed = (
        P(None, "gx", "gy", "gz"),
        P(),
        P(),
        P(),
        P(None, ("gy", "gz"), None, None, None),
        P(),
        P(),
    )
    return jax.shard_map(
        local,
        mesh=mesh,
        in_specs=placed,
        out_specs=(P(None, "gx", "gy", "gz"), P(None, ("gy", "gz"), None, None, None)),
        check_vma=False,
    )
```

```python
import functools
import math

import jax
import jax.numpy as jnp
import ml_dtypes
import numpy as np
from jax import lax
from jax.experimental import pallas as pl
from jax.experimental.pallas import tpu as pltpu
from jax.sharding import PartitionSpec as P

KM = 16
WIN = 32
RATIO = 4

time_step = 0.1
viscosity = 1.0
highest = lax.Precision.HIGHEST


def fourier_angles():
    points = np.arange(WIN)
    freqs = np.arange(KM) - KM // 2
    return 2.0 * math.pi / WIN * ((points[:, None] * freqs[None, :]) % WIN)


def plane_table(parts):
    angle = fourier_angles()
    full = angle.T[:, None, None, :] + angle.T[None, :, :, None]
    full = full.reshape(parts, 1, KM * KM // parts, WIN * WIN)
    both = np.concatenate([np.cos(full), -np.sin(full)], axis=1) * float(WIN) ** (-1.5)
    return both.reshape(2 * KM * KM, WIN * WIN).astype(np.float32)


def line_table():
    angle = fourier_angles()
    table = np.zeros((WIN, 2, KM, 2))
    table[:, 0, :, 0] = np.cos(angle)
    table[:, 0, :, 1] = -np.sin(angle)
    table[:, 1, :, 0] = np.sin(angle)
    table[:, 1, :, 1] = np.cos(angle)
    return table.astype(np.float32)


def halves(table):
    high = table.astype(ml_dtypes.bfloat16)
    low = (table - high.astype(np.float32)).astype(ml_dtypes.bfloat16)
    return jnp.asarray(high), jnp.asarray(low)


def split(values):
    high = values.astype(jnp.bfloat16)
    low = (values - high.astype(jnp.float32)).astype(jnp.bfloat16)
    return high, low


def mul(a, b):
    return jnp.dot(a, b, preferred_element_type=jnp.float32)


def stencil_body(v_ref, x_ref, y_ref, z_ref, out_ref):
    comps, rows, _, length = v_ref.shape
    lane = lax.broadcasted_iota(jnp.int32, v_ref.shape[2:], 1)
    for y in range(rows):
        center = [v_ref[c, y] for c in range(comps)]
        for c in range(comps):
            u = center[c]
            above = x_ref[c, 1, :, y : y + 1]
            below = x_ref[c, 0, :, y : y + 1]
            upper = [
                jnp.where(lane == length - 1, above, pltpu.roll(u, length - 1, 1)),
                v_ref[c, y + 1] if y + 1 < rows else y_ref[c, 1],
                jnp.concatenate([u[1:], z_ref[c, 1, y : y + 1]], axis=0),
            ]
            lower = [
                jnp.where(lane == 0, below, pltpu.roll(u, 1, 1)),
                v_ref[c, y - 1] if y > 0 else y_ref[c, 0],
                jnp.concatenate([z_ref[c, 0, y : y + 1], u[:-1]], axis=0),
            ]
            laplace = upper[0] + lower[0] + upper[1] + lower[1] + upper[2] + lower[2] - 6.0 * u
            carried = (center[0] * (upper[0] - lower[0]) + center[1] * (upper[1] - lower[1])
                       + center[2] * (upper[2] - lower[2]))
            out_ref[c, y] = u + time_step * (viscosity * laplace - 0.5 * carried)


def mix_body(h_ref, w_ref, out_ref):
    for k in range(KM):
        h = h_ref[0, k]
        rows = h.shape[0]
        high = h.astype(jnp.bfloat16).astype(jnp.float32)
        lhs = jnp.concatenate([high, h - high], axis=0).astype(jnp.bfloat16)
        weight = jnp.concatenate([w_ref[0, 0, k], w_ref[1, 0, k]], axis=0)
        both = mul(lhs, weight)
        out_ref[0, k] = both[:rows] + both[rows:]


def middle_body(slots, b_ref, inp_ref, tgt_ref, live_ref, m1_ref, p1_ref, p2_ref,
                bh_ref, bl_ref, fh_ref, fl_ref, out_ref):
    blocks, _, two, modes, lanes = b_ref.shape
    b = b_ref[...].reshape(blocks * two * modes, lanes)
    high, low = split(b)
    pre = mul(bh_ref[...], high) + mul(bh_ref[...], low) + mul(bl_ref[...], high)
    pre = pre + jnp.dot(inp_ref[0], m1_ref[...], precision=highest,
                        preferred_element_type=jnp.float32)
    cdf = 0.5 + 0.5 * lax.erf(pre * math.sqrt(0.5))
    act = pre * cdf
    slope = cdf + pre * (jnp.exp(-0.5 * pre * pre) * (1.0 / math.sqrt(2.0 * math.pi)))
    output = jnp.dot(act, p1_ref[...], precision=highest, preferred_element_type=jnp.float32)
    error = (output - tgt_ref[0]) * live_ref[...]
    grad = jnp.dot(error, p2_ref[...], precision=highest,
                   preferred_element_type=jnp.float32) * slope
    high, low = split(grad)
    cot = mul(fh_ref[...], high) + mul(fh_ref[...], low) + mul(fl_ref[...], high)
    out_ref[...] = cot.reshape(b_ref.shape)


def grad_body(f_ref, l_ref, b_ref, out_ref):
    groups, _, pairs, rows, _ = b_ref.shape
    comps, width, triple = l_ref.shape
    depth = triple // 3
    lane = lax.broadcasted_iota(jnp.int32, (width, triple), 1)
    middle = (lane >= depth) & (lane < 2 * depth)
    row = lax.broadcasted_iota(jnp.int32, (rows, 2 * width), 0)
    sign = jnp.where(row < rows // 2, 1.0, -1.0)
    for pair in range(pairs):
        tiles = [b_ref[g, 0, pair] for g in range(groups)]
        turned = [pltpu.roll(t, rows // 2, 0) * sign for t in tiles]
        rights = []
        for which in (tiles, turned):
            b = jnp.concatenate(which, axis=0)
            high = b.astype(jnp.bfloat16).astype(jnp.float32)
            rights.append(
                jnp.concatenate([high, high, b - high], axis=0).astype(jnp.bfloat16))
        for odd in range(2):
            k = 2 * pair + odd
            a = l_ref[0] * f_ref[0, k, 0:1]
            for c in range(1, comps):
                a = a + l_ref[c] * f_ref[0, k, c : c + 1]
            high = a.astype(jnp.bfloat16).astype(jnp.float32)
            lhs = jnp.where(middle, a - high, high).astype(jnp.bfloat16)
            for c in range(2):
                out_ref[c, 0, k] = mul(lhs, rights[c][:, odd * width : (odd + 1) * width])


def around(x, axis, dim):
    size, length = lax.axis_size(axis), x.shape[dim]
    up = [(i, (i + 1) % size) for i in range(size)]
    down = [(j, i) for i, j in up]
    last = lax.squeeze(lax.slice_in_dim(x, length - 1, length, axis=dim), (dim,))
    first = lax.squeeze(lax.slice_in_dim(x, 0, 1, axis=dim), (dim,))
    return lax.ppermute(last, axis, up), lax.ppermute(first, axis, down)


def coarsen(field):
    comps, ny, nz, nx = field.shape
    lines = field.reshape(comps, ny // RATIO, RATIO, nz, nx).sum(axis=2)
    sum_z = jnp.asarray(np.kron(np.eye(nz // RATIO), np.ones((RATIO, 1))).astype(np.float32))
    sum_x = jnp.asarray(
        np.kron(np.eye(nx // RATIO), np.ones((RATIO, 1))).astype(np.float32) / RATIO**3)
    lines = jnp.einsum("ayzx,xv->ayzv", lines, sum_x, precision=highest)
    return jnp.einsum("ayzv,zu->uyav", lines, sum_z, precision=highest)


def spread(values, axes):
    size = lax.axis_size(axes)
    copies = jnp.broadcast_to(values[None], (size,) + values.shape)
    return lax.all_to_all(copies, axes, split_axis=0, concat_axis=0, tiled=True)


def windows(field, offsets, slots):
    longer = jnp.concatenate([field, field[:WIN]], axis=0)
    return jnp.stack(
        [lax.dynamic_slice_in_dim(longer, offsets[s], WIN, 0) for s in range(slots)])


def local(
    velocity, window_offsets, window_counts, lift_weight, spectral_weight, point_weight, proj_weight
):
    both_axes = ("gy", "gz")
    rows_y, rows_z, groups = lax.axis_size("gy"), lax.axis_size("gz"), lax.axis_size("gx")
    parts = rows_y * rows_z
    part = lax.axis_index("gy") * rows_z + lax.axis_index("gz")
    group = lax.axis_index("gx")
    slots = window_offsets.shape[1]
    width = lift_weight.shape[0]
    lanes = slots * width
    modes = spectral_weight.shape[1]
    planes = WIN // parts
    cells = WIN * WIN
    offsets = lax.dynamic_index_in_dim(window_offsets, group, 0, keepdims=False)
    count = lax.dynamic_index_in_dim(window_counts, group, 0, keepdims=False)
    live = (jnp.arange(slots, dtype=jnp.int32) < count).astype(jnp.float32)
    big = pltpu.CompilerParams(vmem_limit_bytes=48 * 1024 * 1024)
    table = plane_table(parts)
    line = jnp.asarray(line_table())

    turned = jnp.transpose(velocity, (0, 2, 3, 1))
    old = coarsen(turned)
    zl, yl, comps, _ = old.shape
    old = spread(old.reshape(zl, yl, comps * WIN), both_axes)
    old = old.reshape(rows_y, rows_z, zl, yl, comps * WIN)
    old = jnp.transpose(old, (1, 2, 0, 3, 4)).reshape(rows_z * zl, rows_y * yl, comps * WIN)
    seen = windows(old, offsets, slots).reshape(slots, cells, comps * WIN)
    mine = lax.dynamic_index_in_dim(
        jnp.asarray(table).reshape(parts, 2 * modes, cells), part, 0, keepdims=False)
    inner = jnp.einsum("qn,snr->sqr", mine, seen, precision=highest)
    inner = inner.reshape(slots, 2, modes, comps, WIN)
    found = jnp.einsum("xckd,scmax->mkdsa", line, inner, precision=highest)
    found = found.reshape(modes * KM * 2 * slots, comps)
    hid = jnp.einsum("ra,wa->rw", found, lift_weight, precision=highest)
    hid = hid.reshape(modes, KM, 2, slots, width)
    lhs = jnp.concatenate(
        [
            jnp.concatenate([hid[:, :, 0], -hid[:, :, 1]], axis=-1),
            jnp.concatenate([hid[:, :, 1], hid[:, :, 0]], axis=-1),
        ],
        axis=2,
    )
    mixed = pl.pallas_call(
        mix_body,
        grid=(modes,),
        in_specs=[
            pl.BlockSpec((1, KM, 2 * slots, 2 * width), lambda i: (i, 0, 0, 0)),
            pl.BlockSpec((2, 1, KM, width, width), lambda i: (0, i, 0, 0, 0)),
        ],
        out_specs=pl.BlockSpec((1, KM, 2 * slots, width), lambda i: (i, 0, 0, 0)),
        out_shape=jax.ShapeDtypeStruct((modes, KM, 2 * slots, width), jnp.float32),
        compiler_params=big,
    )(lhs, spectral_weight)
    mixed = mixed.reshape(modes, KM, 2, slots, width)
    mixed = jnp.transpose(mixed, (1, 2, 0, 3, 4)).reshape(2 * KM, modes * lanes)
    flat = line.reshape(2 * WIN, 2 * KM)
    back = jnp.dot(flat, mixed, precision=highest)
    pieces = 2 if planes % 2 == 0 else 1
    some = planes // pieces
    back = back.reshape(parts, pieces, some, 2, modes, lanes)
    back = [
        lax.all_to_all(back[:, p], both_axes, split_axis=0, concat_axis=0, tiled=True)
        for p in range(pieces)
    ]

    x_side = jnp.stack(around(jnp.transpose(turned, (0, 2, 1, 3)), "gx", 3), axis=1)
    y_side = jnp.stack(around(turned, "gy", 1), axis=1)
    z_side = jnp.stack(around(turned, "gz", 2), axis=1)
    turned_next = pl.pallas_call(
        stencil_body,
        out_shape=jax.ShapeDtypeStruct(turned.shape, jnp.float32),
        in_specs=[pl.BlockSpec(memory_space=pltpu.VMEM)] * 4,
        out_specs=pl.BlockSpec(memory_space=pltpu.VMEM),
        compiler_params=big,
        cost_estimate=pl.CostEstimate(
            flops=20 * velocity.size, bytes_accessed=8 * velocity.size, transcendentals=0),
    )(turned, x_side, y_side, z_side)
    velocity_next = jnp.transpose(turned_next, (0, 3, 1, 2))
    new = coarsen(turned_next)
    new = new.reshape(zl, yl, comps, parts, planes)
    new = jnp.transpose(new, (3, 0, 1, 2, 4)).reshape(parts, zl, yl, comps * planes)
    new = lax.all_to_all(new, both_axes, split_axis=0, concat_axis=0, tiled=True)
    new = new.reshape(rows_y, rows_z, zl, yl, comps * planes)
    new = jnp.transpose(new, (1, 2, 0, 3, 4)).reshape(rows_z * zl, rows_y * yl, comps * planes)

    def by_plane(values):
        values = values.reshape(slots, cells, comps, planes)
        return jnp.transpose(values, (3, 1, 0, 2)).reshape(planes, cells, slots * comps)

    targets = by_plane(windows(new, offsets, slots))
    own = lax.dynamic_slice_in_dim(
        seen.reshape(slots, cells, comps, WIN), part * planes, planes, 3)
    inputs = by_plane(own)

    eye = jnp.eye(slots, dtype=jnp.float32)
    point = jnp.dot(point_weight, lift_weight, precision=highest)
    m1 = jnp.einsum("st,oc->scto", eye, point, precision=highest).reshape(slots * comps, lanes)
    p2 = jnp.einsum("st,co->scto", eye, proj_weight, precision=highest)
    p2 = p2.reshape(slots * comps, lanes)
    alive = jnp.repeat(live, comps)[None]
    forward_high, forward_low = halves(table)
    back_high, back_low = halves(np.ascontiguousarray(table.T))

    def whole(shape):
        return pl.BlockSpec(shape, lambda i: (0,) * len(shape))

    every = spread(found.reshape(modes, KM, 2, slots, comps), "gx")
    depth = groups * 2 * slots
    every = jnp.transpose(every, (1, 2, 5, 0, 3, 4)).reshape(modes, KM, comps, depth)
    every = jnp.concatenate([every, every, every], axis=-1)
    back, every = lax.optimization_barrier((back, every))

    sc = slots * comps
    mode_spec = pl.BlockSpec((parts, 1, 2, modes, lanes), lambda i: (0, i, 0, 0, 0))
    full_modes = 2 * modes * parts
    by_part = line.reshape(parts, pieces, some, 2, 2 * KM)
    cot = 0.0
    for p in range(pieces):
        plane_spec = pl.BlockSpec((1, cells, sc), lambda i, p=p: (i + p * some, 0, 0))
        piece = pl.pallas_call(
            functools.partial(middle_body, slots),
            grid=(some,),
            in_specs=[
                mode_spec, plane_spec, plane_spec, whole((1, sc)), whole((sc, lanes)),
                whole((lanes, sc)), whole((sc, lanes)), whole((cells, full_modes)),
                whole((cells, full_modes)), whole((full_modes, cells)),
                whole((full_modes, cells)),
            ],
            out_specs=mode_spec,
            out_shape=jax.ShapeDtypeStruct(back[p].shape, jnp.float32),
            compiler_params=big,
            cost_estimate=pl.CostEstimate(
                flops=12 * some * cells * full_modes * lanes,
                bytes_accessed=8 * some * full_modes * lanes,
                transcendentals=2 * some * cells * lanes),
        )(back[p], inputs, targets, alive, m1, p2.T, p2, back_high, back_low, forward_high,
          forward_low)
        piece = lax.all_to_all(piece, both_axes, split_axis=0, concat_axis=0, tiled=True)
        rows = by_part[:, p].reshape(parts * some * 2, 2 * KM)
        cot = cot + jnp.dot(
            rows.T, piece.reshape(parts * some * 2, modes * lanes), precision=highest)

    cot = cot.reshape(KM // 2, 2, 2, modes, slots, width)
    cot = jnp.transpose(cot, (3, 0, 2, 4, 1, 5)).reshape(modes, KM // 2, 2 * slots, 2 * width)
    right = lax.all_gather(cot, "gx")
    lifts = jnp.broadcast_to(lift_weight.T[:, :, None], (comps, width, 3 * depth))
    grad_spectral = pl.pallas_call(
        grad_body,
        grid=(modes,),
        in_specs=[
            pl.BlockSpec((1, KM, comps, 3 * depth), lambda i: (i, 0, 0, 0)),
            whole((comps, width, 3 * depth)),
            pl.BlockSpec((groups, 1, KM // 2, 2 * slots, 2 * width),
                         lambda i: (0, i, 0, 0, 0)),
        ],
        out_specs=pl.BlockSpec((2, 1, KM, width, width), lambda i: (0, i, 0, 0, 0)),
        out_shape=jax.ShapeDtypeStruct((2, modes, KM, width, width), jnp.float32),
        compiler_params=big,
    )(every, lifts, right)
    return (velocity_next, grad_spectral)


def solution(mesh):
    placed = (
        P(None, "gx", "gy", "gz"),
        P(),
        P(),
        P(),
        P(None, ("gy", "gz"), None, None, None),
        P(),
        P(),
    )
    return jax.shard_map(
        local,
        mesh=mesh,
        in_specs=placed,
        out_specs=(P(None, "gx", "gy", "gz"), P(None, ("gy", "gz"), None, None, None)),
        check_vma=False,
    )
```

```python
import functools
import math

import jax
import jax.numpy as jnp
import ml_dtypes
import numpy as np
from jax import lax
from jax.experimental import pallas as pl
from jax.experimental.pallas import tpu as pltpu
from jax.sharding import PartitionSpec as P

KM = 16
WIN = 32
RATIO = 4

time_step = 0.1
viscosity = 1.0
highest = lax.Precision.HIGHEST


def fourier_angles():
    points = np.arange(WIN)
    freqs = np.arange(KM) - KM // 2
    return 2.0 * math.pi / WIN * ((points[:, None] * freqs[None, :]) % WIN)


def plane_table(parts):
    angle = fourier_angles()
    full = angle.T[:, None, None, :] + angle.T[None, :, :, None]
    full = full.reshape(parts, 1, KM * KM // parts, WIN * WIN)
    both = np.concatenate([np.cos(full), -np.sin(full)], axis=1) * float(WIN) ** (-1.5)
    return both.reshape(2 * KM * KM, WIN * WIN).astype(np.float32)


def line_table():
    angle = fourier_angles()
    table = np.zeros((WIN, 2, KM, 2))
    table[:, 0, :, 0] = np.cos(angle)
    table[:, 0, :, 1] = -np.sin(angle)
    table[:, 1, :, 0] = np.sin(angle)
    table[:, 1, :, 1] = np.cos(angle)
    return table.astype(np.float32)


def halves(table):
    high = table.astype(ml_dtypes.bfloat16)
    low = (table - high.astype(np.float32)).astype(ml_dtypes.bfloat16)
    return jnp.asarray(high), jnp.asarray(low)


def split(values):
    high = values.astype(jnp.bfloat16)
    low = (values - high.astype(jnp.float32)).astype(jnp.bfloat16)
    return high, low


def mul(a, b):
    return jnp.dot(a, b, preferred_element_type=jnp.float32)


def stencil_body(v_ref, x_ref, y_ref, z_ref, out_ref):
    comps, rows, _, length = v_ref.shape
    lane = lax.broadcasted_iota(jnp.int32, v_ref.shape[2:], 1)
    for y in range(rows):
        center = [v_ref[c, y] for c in range(comps)]
        for c in range(comps):
            u = center[c]
            above = x_ref[c, 1, :, y : y + 1]
            below = x_ref[c, 0, :, y : y + 1]
            upper = [
                jnp.where(lane == length - 1, above, pltpu.roll(u, length - 1, 1)),
                v_ref[c, y + 1] if y + 1 < rows else y_ref[c, 1],
                jnp.concatenate([u[1:], z_ref[c, 1, y : y + 1]], axis=0),
            ]
            lower = [
                jnp.where(lane == 0, below, pltpu.roll(u, 1, 1)),
                v_ref[c, y - 1] if y > 0 else y_ref[c, 0],
                jnp.concatenate([z_ref[c, 0, y : y + 1], u[:-1]], axis=0),
            ]
            laplace = upper[0] + lower[0] + upper[1] + lower[1] + upper[2] + lower[2] - 6.0 * u
            carried = (center[0] * (upper[0] - lower[0]) + center[1] * (upper[1] - lower[1])
                       + center[2] * (upper[2] - lower[2]))
            out_ref[c, y] = u + time_step * (viscosity * laplace - 0.5 * carried)


def mix_body(h_ref, w_ref, out_ref):
    for k in range(KM):
        h = h_ref[0, k]
        rows = h.shape[0]
        high = h.astype(jnp.bfloat16).astype(jnp.float32)
        lhs = jnp.concatenate([high, h - high], axis=0).astype(jnp.bfloat16)
        weight = jnp.concatenate([w_ref[0, 0, k], w_ref[1, 0, k]], axis=0)
        both = mul(lhs, weight)
        out_ref[0, k] = both[:rows] + both[rows:]


def middle_body(slots, b_ref, inp_ref, tgt_ref, live_ref, m1_ref, p1_ref, p2_ref,
                bh_ref, bl_ref, fh_ref, fl_ref, out_ref):
    blocks, _, two, modes, lanes = b_ref.shape
    b = b_ref[...].reshape(blocks * two * modes, lanes)
    high, low = split(b)
    pre = mul(bh_ref[...], high) + mul(bh_ref[...], low) + mul(bl_ref[...], high)
    pre = pre + jnp.dot(inp_ref[0], m1_ref[...], precision=highest,
                        preferred_element_type=jnp.float32)
    cdf = 0.5 + 0.5 * lax.erf(pre * math.sqrt(0.5))
    act = pre * cdf
    slope = cdf + pre * (jnp.exp(-0.5 * pre * pre) * (1.0 / math.sqrt(2.0 * math.pi)))
    output = jnp.dot(act, p1_ref[...], precision=highest, preferred_element_type=jnp.float32)
    error = (output - tgt_ref[0]) * live_ref[...]
    grad = jnp.dot(error, p2_ref[...], precision=highest,
                   preferred_element_type=jnp.float32) * slope
    high, low = split(grad)
    cot = mul(fh_ref[...], high) + mul(fh_ref[...], low) + mul(fl_ref[...], high)
    out_ref[...] = cot.reshape(b_ref.shape)


def grad_body(f_ref, l_ref, b0_ref, b1_ref, out_ref):
    groups, _, pairs, rows, _ = b0_ref.shape
    comps, width, triple = l_ref.shape
    depth = triple // 3
    lane = lax.broadcasted_iota(jnp.int32, (width, triple), 1)
    middle = (lane >= depth) & (lane < 2 * depth)
    row = lax.broadcasted_iota(jnp.int32, (rows, 2 * width), 0)
    sign = jnp.where(row < rows // 2, 1.0, -1.0)
    for pair in range(2 * pairs):
        b_ref = b0_ref if pair < pairs else b1_ref
        tiles = [b_ref[g, 0, pair % pairs] for g in range(groups)]
        turned = [pltpu.roll(t, rows // 2, 0) * sign for t in tiles]
        rights = []
        for which in (tiles, turned):
            b = jnp.concatenate(which, axis=0)
            high = b.astype(jnp.bfloat16).astype(jnp.float32)
            rights.append(
                jnp.concatenate([high, high, b - high], axis=0).astype(jnp.bfloat16))
        for odd in range(2):
            k = 2 * pair + odd
            a = l_ref[0] * f_ref[0, k, 0:1]
            for c in range(1, comps):
                a = a + l_ref[c] * f_ref[0, k, c : c + 1]
            high = a.astype(jnp.bfloat16).astype(jnp.float32)
            lhs = jnp.where(middle, a - high, high).astype(jnp.bfloat16)
            for c in range(2):
                out_ref[c, 0, k] = mul(lhs, rights[c][:, odd * width : (odd + 1) * width])


def around(x, axis, dim):
    size, length = lax.axis_size(axis), x.shape[dim]
    up = [(i, (i + 1) % size) for i in range(size)]
    down = [(j, i) for i, j in up]
    last = lax.squeeze(lax.slice_in_dim(x, length - 1, length, axis=dim), (dim,))
    first = lax.squeeze(lax.slice_in_dim(x, 0, 1, axis=dim), (dim,))
    return lax.ppermute(last, axis, up), lax.ppermute(first, axis, down)


def coarsen(field):
    comps, ny, nz, nx = field.shape
    lines = field.reshape(comps, ny // RATIO, RATIO, nz, nx).sum(axis=2)
    sum_z = jnp.asarray(np.kron(np.eye(nz // RATIO), np.ones((RATIO, 1))).astype(np.float32))
    sum_x = jnp.asarray(
        np.kron(np.eye(nx // RATIO), np.ones((RATIO, 1))).astype(np.float32) / RATIO**3)
    lines = jnp.einsum("ayzx,xv->ayzv", lines, sum_x, precision=highest)
    return jnp.einsum("ayzv,zu->uyav", lines, sum_z, precision=highest)


def spread(values, axes):
    size = lax.axis_size(axes)
    copies = jnp.broadcast_to(values[None], (size,) + values.shape)
    return lax.all_to_all(copies, axes, split_axis=0, concat_axis=0, tiled=True)


def windows(field, offsets, slots):
    longer = jnp.concatenate([field, field[:WIN]], axis=0)
    return jnp.stack(
        [lax.dynamic_slice_in_dim(longer, offsets[s], WIN, 0) for s in range(slots)])


def local(
    velocity, window_offsets, window_counts, lift_weight, spectral_weight, point_weight, proj_weight
):
    both_axes = ("gy", "gz")
    rows_y, rows_z, groups = lax.axis_size("gy"), lax.axis_size("gz"), lax.axis_size("gx")
    parts = rows_y * rows_z
    part = lax.axis_index("gy") * rows_z + lax.axis_index("gz")
    group = lax.axis_index("gx")
    slots = window_offsets.shape[1]
    width = lift_weight.shape[0]
    lanes = slots * width
    modes = spectral_weight.shape[1]
    planes = WIN // parts
    cells = WIN * WIN
    offsets = lax.dynamic_index_in_dim(window_offsets, group, 0, keepdims=False)
    count = lax.dynamic_index_in_dim(window_counts, group, 0, keepdims=False)
    live = (jnp.arange(slots, dtype=jnp.int32) < count).astype(jnp.float32)
    big = pltpu.CompilerParams(vmem_limit_bytes=48 * 1024 * 1024)
    table = plane_table(parts)
    line = jnp.asarray(line_table())

    turned = jnp.transpose(velocity, (0, 2, 3, 1))
    old = coarsen(turned)
    zl, yl, comps, _ = old.shape
    old = spread(old.reshape(zl, yl, comps * WIN), both_axes)
    old = old.reshape(rows_y, rows_z, zl, yl, comps * WIN)
    old = jnp.transpose(old, (1, 2, 0, 3, 4)).reshape(rows_z * zl, rows_y * yl, comps * WIN)
    seen = windows(old, offsets, slots).reshape(slots, cells, comps * WIN)
    mine = lax.dynamic_index_in_dim(
        jnp.asarray(table).reshape(parts, 2 * modes, cells), part, 0, keepdims=False)
    inner = jnp.einsum("qn,snr->sqr", mine, seen, precision=highest)
    inner = inner.reshape(slots, 2, modes, comps, WIN)
    found = jnp.einsum("xckd,scmax->mkdsa", line, inner, precision=highest)
    found = found.reshape(modes * KM * 2 * slots, comps)
    hid = jnp.einsum("ra,wa->rw", found, lift_weight, precision=highest)
    hid = hid.reshape(modes, KM, 2, slots, width)
    lhs = jnp.concatenate(
        [
            jnp.concatenate([hid[:, :, 0], -hid[:, :, 1]], axis=-1),
            jnp.concatenate([hid[:, :, 1], hid[:, :, 0]], axis=-1),
        ],
        axis=2,
    )
    mixed = pl.pallas_call(
        mix_body,
        grid=(modes,),
        in_specs=[
            pl.BlockSpec((1, KM, 2 * slots, 2 * width), lambda i: (i, 0, 0, 0)),
            pl.BlockSpec((2, 1, KM, width, width), lambda i: (0, i, 0, 0, 0)),
        ],
        out_specs=pl.BlockSpec((1, KM, 2 * slots, width), lambda i: (i, 0, 0, 0)),
        out_shape=jax.ShapeDtypeStruct((modes, KM, 2 * slots, width), jnp.float32),
        compiler_params=big,
    )(lhs, spectral_weight)
    y_side = jnp.stack(around(turned, "gy", 1), axis=1)
    mixed, y_side = lax.optimization_barrier((mixed, y_side))
    mixed = mixed.reshape(modes, KM, 2, slots, width)
    mixed = jnp.transpose(mixed, (1, 2, 0, 3, 4)).reshape(2 * KM, modes * lanes)
    flat = line.reshape(2 * WIN, 2 * KM)
    back = jnp.dot(flat, mixed, precision=highest)
    pieces = 2 if planes % 2 == 0 else 1
    some = planes // pieces
    back = back.reshape(parts, pieces, some, 2, modes, lanes)
    back = [
        lax.all_to_all(back[:, p], both_axes, split_axis=0, concat_axis=0, tiled=True)
        for p in range(pieces)
    ]

    x_side = jnp.stack(around(jnp.transpose(turned, (0, 2, 1, 3)), "gx", 3), axis=1)
    z_side = jnp.stack(around(turned, "gz", 2), axis=1)
    turned_next = pl.pallas_call(
        stencil_body,
        out_shape=jax.ShapeDtypeStruct(turned.shape, jnp.float32),
        in_specs=[pl.BlockSpec(memory_space=pltpu.VMEM)] * 4,
        out_specs=pl.BlockSpec(memory_space=pltpu.VMEM),
        compiler_params=big,
        cost_estimate=pl.CostEstimate(
            flops=20 * velocity.size, bytes_accessed=8 * velocity.size, transcendentals=0),
    )(turned, x_side, y_side, z_side)
    velocity_next = jnp.transpose(turned_next, (0, 3, 1, 2))
    new = coarsen(turned_next)
    new = new.reshape(zl, yl, comps, parts, planes)
    new = jnp.transpose(new, (3, 0, 1, 2, 4)).reshape(parts, zl, yl, comps * planes)
    new = lax.all_to_all(new, both_axes, split_axis=0, concat_axis=0, tiled=True)
    new = new.reshape(rows_y, rows_z, zl, yl, comps * planes)
    new = jnp.transpose(new, (1, 2, 0, 3, 4)).reshape(rows_z * zl, rows_y * yl, comps * planes)

    def by_plane(values):
        values = values.reshape(slots, cells, comps, planes)
        return jnp.transpose(values, (3, 1, 0, 2)).reshape(planes, cells, slots * comps)

    targets = by_plane(windows(new, offsets, slots))
    own = lax.dynamic_slice_in_dim(
        seen.reshape(slots, cells, comps, WIN), part * planes, planes, 3)
    inputs = by_plane(own)

    eye = jnp.eye(slots, dtype=jnp.float32)
    point = jnp.dot(point_weight, lift_weight, precision=highest)
    m1 = jnp.einsum("st,oc->scto", eye, point, precision=highest).reshape(slots * comps, lanes)
    p2 = jnp.einsum("st,co->scto", eye, proj_weight, precision=highest)
    p2 = p2.reshape(slots * comps, lanes)
    alive = jnp.repeat(live, comps)[None]
    forward_high, forward_low = halves(table)
    back_high, back_low = halves(np.ascontiguousarray(table.T))

    def whole(shape):
        return pl.BlockSpec(shape, lambda i: (0,) * len(shape))

    every = spread(found.reshape(modes, KM, 2, slots, comps), "gx")
    depth = groups * 2 * slots
    every = jnp.transpose(every, (1, 2, 5, 0, 3, 4)).reshape(modes, KM, comps, depth)
    every = jnp.concatenate([every, every, every], axis=-1)
    back, every = lax.optimization_barrier((back, every))

    sc = slots * comps
    mode_spec = pl.BlockSpec((parts, 1, 2, modes, lanes), lambda i: (0, i, 0, 0, 0))
    full_modes = 2 * modes * parts
    by_part = line.reshape(parts, pieces, some, 2, 2 * KM)
    cot = 0.0
    for p in range(pieces):
        plane_spec = pl.BlockSpec((1, cells, sc), lambda i, p=p: (i + p * some, 0, 0))
        piece = pl.pallas_call(
            functools.partial(middle_body, slots),
            grid=(some,),
            in_specs=[
                mode_spec, plane_spec, plane_spec, whole((1, sc)), whole((sc, lanes)),
                whole((lanes, sc)), whole((sc, lanes)), whole((cells, full_modes)),
                whole((cells, full_modes)), whole((full_modes, cells)),
                whole((full_modes, cells)),
            ],
            out_specs=mode_spec,
            out_shape=jax.ShapeDtypeStruct(back[p].shape, jnp.float32),
            compiler_params=big,
            cost_estimate=pl.CostEstimate(
                flops=12 * some * cells * full_modes * lanes,
                bytes_accessed=8 * some * full_modes * lanes,
                transcendentals=2 * some * cells * lanes),
        )(back[p], inputs, targets, alive, m1, p2.T, p2, back_high, back_low, forward_high,
          forward_low)
        piece = lax.all_to_all(piece, both_axes, split_axis=0, concat_axis=0, tiled=True)
        rows = by_part[:, p].reshape(parts * some * 2, 2 * KM)
        cot = cot + jnp.dot(
            rows.T, piece.reshape(parts * some * 2, modes * lanes), precision=highest)

    cot = cot.reshape(KM // 2, 2, 2, modes, slots, width)
    cot = jnp.transpose(cot, (3, 0, 2, 4, 1, 5)).reshape(modes, KM // 2, 2 * slots, 2 * width)
    right = [lax.all_gather(cot[:, : KM // 4], "gx"), lax.all_gather(cot[:, KM // 4 :], "gx")]
    right_spec = pl.BlockSpec(
        (groups, 1, KM // 4, 2 * slots, 2 * width), lambda i: (0, i, 0, 0, 0))
    lifts = jnp.broadcast_to(lift_weight.T[:, :, None], (comps, width, 3 * depth))
    grad_spectral = pl.pallas_call(
        grad_body,
        grid=(modes,),
        in_specs=[
            pl.BlockSpec((1, KM, comps, 3 * depth), lambda i: (i, 0, 0, 0)),
            whole((comps, width, 3 * depth)),
            right_spec,
            right_spec,
        ],
        out_specs=pl.BlockSpec((2, 1, KM, width, width), lambda i: (0, i, 0, 0, 0)),
        out_shape=jax.ShapeDtypeStruct((2, modes, KM, width, width), jnp.float32),
        compiler_params=big,
    )(every, lifts, *right)
    return (velocity_next, grad_spectral)


def solution(mesh):
    placed = (
        P(None, "gx", "gy", "gz"),
        P(),
        P(),
        P(),
        P(None, ("gy", "gz"), None, None, None),
        P(),
        P(),
    )
    return jax.shard_map(
        local,
        mesh=mesh,
        in_specs=placed,
        out_specs=(P(None, "gx", "gy", "gz"), P(None, ("gy", "gz"), None, None, None)),
        check_vma=False,
    )
```
